256 devices in a mesh: ctx: 32 (over z_lo, x, core), tp: 8 (over y, z_hi).
Axes of the slice: x: 4, y: 4, z: 8 (z_hi: 2, z_lo: 4; z = z_hi * 4 + z_lo), core: 2. Of those that a mesh axis runs over, the one named last changes fastest.
Arguments:
- out_cotangent: bfloat16 [4096, 8192], P('tp', 'ctx'), may hold values from -4 to 4
- query_rows: bfloat16 [4096, 8192], P('tp', 'ctx'), may hold values from -6 to 6
- key_rows: bfloat16 [4096, 8192], P('tp', 'ctx'), may hold values from -6 to 6
- value_rows: bfloat16 [4096, 8192], P('tp', 'ctx'), may hold values from -6 to 6
- long_filter: float32 [4096, 8192], P('tp', 'ctx'), may hold values from -0.0625 to 0.0625
- short_filter: float32 [3, 4096, 7], P(None, 'tp'), may hold values from -3 to 3
- out_weight: bfloat16 [4096, 4096], P(None, 'tp'), may hold values from -0.09375 to 0.09375
Outputs:
- feature_grad: bfloat16 [3, 4096, 8192], P(None, 'tp', 'ctx')
- filter_grad: float32 [4096, 8192], P('tp', 'ctx')
- out_weight_grad: float32 [4096, 4096], P('ctx', 'tp')
The draws below stay inside these ranges and needn't reach their ends.
All inputs are finite; a program needn't handle non-finite values.
Results may differ from the reference program's by a relative error of at most 0.03.
Values may be sent and summed in bfloat16 or wider, within the bound.
No kernel may reach another device: no remote copies, remote signals or barrier semaphores. Data moves between devices by JAX's collectives and lax.ppermute only.
A program may use at most 64 MiB of HBM per device.

```python
import jax
import jax.numpy as jnp
from jax import lax

D = 4096
SHORT = 7
SLAB = 8192


def with_spikes(values, rng, source, target, blocks, factor):
    def block_of(dim):
        return (jnp.arange(values.shape[dim]) // (values.shape[dim] // blocks)).reshape((-1,) + (1,) * (values.ndim - 1 - dim))

    one_side = jax.random.permutation(rng, blocks)[block_of(target)]
    far = (block_of(target) + blocks // 2) % blocks
    return jnp.where((block_of(source) == one_side) | (block_of(source) == far), factor * values, values)


def level_of(own_key, shape, cuts, low, top_value):
    factor_of, own = 1.0, jax.random.fold_in(own_key, 6)
    for position, shards_of in cuts:
        steps = jnp.exp(jax.random.uniform(jax.random.fold_in(own, position), (shards_of,), jnp.float32, low / len(cuts), top_value / len(cuts)))
        factor_of = factor_of * jnp.repeat(steps, shape[position] // shards_of).reshape([-1 if axis == position else 1 for axis in range(len(shape))])
    return factor_of


def bell_draw(key, extent, deviation, reach, pieces=(), kind=jnp.bfloat16):
    result = jax.random.normal(key, extent, jnp.float32) * deviation
    if len(pieces) > 0:
        result = level_of(key, extent, pieces, -0.22, 0.18) * result
    return jnp.clip(result, min=-reach, max=reach).astype(kind)


def heavy_noise(rng, shape, deviation, limit, split, heavy, held_as=jnp.bfloat16):
    result = deviation * jax.random.normal(rng, shape, jnp.float32)
    if split:
        result = result * level_of(rng, shape, split, -0.22, 0.18)
    return jnp.clip(with_spikes(result, jax.random.fold_in(rng, 3), *heavy), -limit, limit).astype(held_as)


def setup_inputs(seed: int = 0) -> dict:
    streams_of = jax.random.split(jax.random.key(seed), 8)
    return {
        "out_cotangent": heavy_noise(streams_of[0], (D, SLAB), 0.5, 4.0, ((0, 8), (1, 32)), (1, 0, 32, 2.75)),
        "query_rows": bell_draw(streams_of[1], (D, SLAB), 1.0, 6.0, ((0, 8), (1, 32))),
        "key_rows": bell_draw(streams_of[2], (D, SLAB), 1.0, 6.0, ((0, 8), (1, 32))),
        "value_rows": bell_draw(streams_of[3], (D, SLAB), 1.0, 6.0, ((0, 8), (1, 32))),
        "long_filter": bell_draw(streams_of[4], (D, SLAB), SLAB ** -0.5, 0.0625, ((0, 8), (1, 32)), jnp.float32),
        "short_filter": bell_draw(streams_of[5], (3, D, SHORT), 0.5, 3.0, ((1, 8),), jnp.float32),
        "out_weight": bell_draw(streams_of[6], (D, D), D ** -0.5, 0.09375, ((1, 8),)),
    }


def long_terms(blocks):
    kv_block, gated_block, filter_block = blocks
    length = kv_block.shape[-1]
    total = 2 * length
    kv_spec = jnp.fft.rfft(kv_block, n=total, axis=-1)
    gated_spec = jnp.fft.rfft(gated_block, n=total, axis=-1)
    filter_spec = jnp.fft.rfft(filter_block, n=total, axis=-1)
    conv_full = jnp.fft.irfft(filter_spec * kv_spec, n=total, axis=-1)[:, :length]
    adjoint_full = jnp.fft.irfft(jnp.conj(filter_spec) * gated_spec, n=total, axis=-1)[:, :length]
    corr_full = jnp.fft.irfft(gated_spec * jnp.conj(kv_spec), n=total, axis=-1)[:, :length]
    return conv_full.astype(kv_block.dtype), adjoint_full.astype(kv_block.dtype), corr_full.astype(kv_block.dtype)


def reference(out_cotangent, query_rows, key_rows, value_rows, long_filter, short_filter, out_weight):
    inner_grad = jnp.dot(out_weight.T, out_cotangent, preferred_element_type=jnp.float32).astype(jnp.bfloat16)
    kv_product = (key_rows.astype(jnp.float32) * value_rows.astype(jnp.float32)).astype(jnp.bfloat16)
    gated = (inner_grad.astype(jnp.float32) * query_rows.astype(jnp.float32)).astype(jnp.bfloat16)
    width = kv_product.shape[0]
    length = kv_product.shape[1]
    blocks_count = width // 256
    kv_blocks = kv_product.astype(jnp.float32).reshape(blocks_count, 256, length)
    gated_blocks = gated.astype(jnp.float32).reshape(blocks_count, 256, length)
    filter_blocks = long_filter.astype(jnp.float32).reshape(blocks_count, 256, length)
    conv_full, adjoint_full, corr_full = lax.map(long_terms, (kv_blocks, gated_blocks, filter_blocks))
    conv_out = conv_full.reshape(width, length).astype(jnp.bfloat16)
    kv_grad = adjoint_full.reshape(width, length).astype(jnp.bfloat16)
    filter_grad = corr_full.reshape(width, length).astype(jnp.float32)
    conv_wide = conv_out.astype(jnp.float32)
    mixed_inner = (query_rows.astype(jnp.float32) * conv_wide).astype(jnp.bfloat16)
    kv_wide = kv_grad.astype(jnp.float32)
    q_grad = (inner_grad.astype(jnp.float32) * conv_wide).astype(jnp.bfloat16)
    k_grad = (kv_wide * value_rows.astype(jnp.float32)).astype(jnp.bfloat16)
    v_grad = (kv_wide * key_rows.astype(jnp.float32)).astype(jnp.bfloat16)
    post_grad = jnp.stack([q_grad, k_grad, v_grad]).astype(jnp.float32)
    taps = short_filter.shape[2]
    padded = jnp.pad(post_grad, ((0, 0), (0, 0), (0, taps - 1)))
    summed = jnp.zeros(post_grad.shape, jnp.float32)
    for offset in range(taps):
        summed = summed + short_filter[:, :, offset][:, :, None] * padded[:, :, offset:offset + length]
    feature_grad = summed.astype(jnp.bfloat16)
    out_weight_grad = jnp.dot(out_cotangent, mixed_inner.T, preferred_element_type=jnp.float32)
    return feature_grad, filter_grad, out_weight_grad
```

```python
import math

import jax
import jax.numpy as jnp
import ml_dtypes
import numpy as np
from jax import lax
from jax.experimental import pallas as pl
from jax.experimental.pallas import tpu as pltpu
from jax.sharding import PartitionSpec as P

BF = jnp.bfloat16
F32 = jnp.float32
NX, NZ, NY = 4, 4, 4
CTX, TP = 32, 8
CH = 16
LOC = 256
ROWS = 512
KP = 72
FINE = 128
TOTAL = 16384
VMEM = 44 * 1024 * 1024


def ctx_shift(dz, dx, dc):
    return [
        (z * 8 + x * 2 + c, (z + dz) % 4 * 8 + (x + dx) % 4 * 2 + (c + dc) % 2)
        for z in range(4)
        for x in range(4)
        for c in range(2)
    ]


def tp_shift(dy, dh):
    return [(y * 2 + h, (y + dy) % 4 * 2 + (h + dh) % 2) for y in range(4) for h in range(2)]


def split_np(table):
    high = table.astype(ml_dtypes.bfloat16)
    low = (table - high.astype(np.float64)).astype(ml_dtypes.bfloat16)
    return high, low


def make_tables():
    freq = np.arange(KP)[:, None]
    live = (freq <= 64).astype(np.float64)
    coarse = (2 * np.arange(32)[None, :] + np.arange(2)[:, None]).reshape(1, 64)
    angle = 2 * math.pi * ((freq * coarse) % 128) / 128
    first = np.concatenate([np.cos(angle) * live, -np.sin(angle) * live], 0)
    first = np.concatenate(split_np(first), 1)
    fine = np.arange(FINE)
    mid_angle = 2 * math.pi * ((fine[:, None] * fine[None, :]) % 128) / 128
    cos, sin = np.cos(mid_angle), np.sin(mid_angle)
    forward = np.stack(split_np(np.block([[cos, -sin], [sin, cos]])))
    inverse = np.stack(split_np(np.block([[cos, sin], [-sin, cos]])))
    tw_angle = 2 * math.pi * (freq * fine[None, :]) / TOTAL
    twiddle = np.stack([np.cos(tw_angle), np.sin(tw_angle)]).astype(np.float32)
    weight = np.where((freq == 0) | (freq == 64), 1.0, 2.0) * live / TOTAL
    last = np.concatenate([(np.cos(angle) * weight).T, (-np.sin(angle) * weight).T], 1)
    last = np.stack(split_np(last))
    return first, forward, inverse, twiddle, last


def halves(value):
    high = value.astype(BF)
    return high, (value - high.astype(F32)).astype(BF)


def mm(left, right):
    return jnp.dot(left, right, preferred_element_type=F32)


def mm_table(value, table_ref):
    high, low = halves(value)
    return mm(high, table_ref[0]) + mm(low, table_ref[0]) + mm(high, table_ref[1])


def forward_spectrum(block, first_ref, forward_ref, twiddle_ref, work_ref, spec_ref):
    chans = jnp.swapaxes(block.astype(F32), 0, 1).astype(BF)
    cos_tw, sin_tw = twiddle_ref[0], twiddle_ref[1]
    for pair in range(CH // 2):
        cols = []
        for chan in (2 * pair, 2 * pair + 1):
            both = jnp.concatenate([chans[chan, :, :FINE], chans[chan, :, FINE:]], 0)
            cols.append(jnp.concatenate([both, both], 0))
        coarse = mm(first_ref[...], jnp.concatenate(cols, 1))
        for which in range(2):
            real = coarse[:KP, which * FINE : (which + 1) * FINE]
            imag = coarse[KP:, which * FINE : (which + 1) * FINE]
            row = (2 * pair + which) * KP
            work_ref[row : row + KP, :FINE] = real * cos_tw + imag * sin_tw
            work_ref[row : row + KP, FINE:] = imag * cos_tw - real * sin_tw
    spec_ref[...] = mm_table(work_ref[...], forward_ref)


def inverse_signal(work_ref, inverse_ref, twiddle_ref, last_ref):
    work_ref[...] = mm_table(work_ref[...], inverse_ref)
    cos_tw, sin_tw = twiddle_ref[0], twiddle_ref[1]
    chans = []
    for pair in range(CH // 2):
        cols = []
        for chan in (2 * pair, 2 * pair + 1):
            real = work_ref[chan * KP : (chan + 1) * KP, :FINE]
            imag = work_ref[chan * KP : (chan + 1) * KP, FINE:]
            cols.append(
                jnp.concatenate(
                    [real * cos_tw - imag * sin_tw, imag * cos_tw + real * sin_tw], 0
                )
            )
        high, low = halves(jnp.concatenate(cols, 1))
        out = mm(last_ref[0], high) + mm(last_ref[0], low) + mm(last_ref[1], high)
        for which in range(2):
            mine = out[:, which * FINE : (which + 1) * FINE]
            chans.append(jnp.concatenate([mine[:32], mine[32:]], 1))
    return jnp.swapaxes(jnp.stack(chans, 0), 0, 1)


def times(left_ref, right_ref, sign_left, out_ref):
    lr, li = left_ref[:, :FINE], left_ref[:, FINE:]
    rr, ri = right_ref[:, :FINE], right_ref[:, FINE:]
    if sign_left > 0:
        out_ref[:, :FINE] = lr * rr - li * ri
        out_ref[:, FINE:] = lr * ri + li * rr
    else:
        out_ref[:, :FINE] = lr * rr + li * ri
        out_ref[:, FINE:] = lr * ri - li * rr


def prep_kernel(key_ref, value_ref, filter_ref, out_ref):
    kv = (key_ref[...].astype(F32) * value_ref[...].astype(F32)).astype(BF)
    out_ref[:, 0] = kv.reshape(CTX, CH, LOC)
    out_ref[:, 1] = filter_ref[...].astype(BF).reshape(CTX, CH, LOC)


def conv_kernel(in_ref, first, forward, inverse, twiddle, last, out_ref, kv_spec, fil_spec, work):
    forward_spectrum(in_ref[:, 0], first, forward, twiddle, work, kv_spec)
    forward_spectrum(in_ref[:, 1], first, forward, twiddle, work, fil_spec)
    times(fil_spec, kv_spec, 1, work)
    out_ref[...] = inverse_signal(work, inverse, twiddle, last).astype(BF)


def grad_kernel(
    in_ref, kv_spec, fil_spec, first, forward, inverse, twiddle, last, out_ref, spec, work
):
    forward_spectrum(in_ref[...], first, forward, twiddle, work, spec)
    times(fil_spec, spec, -1, work)
    out_ref[:, 0] = inverse_signal(work, inverse, twiddle, last).astype(BF)
    times(kv_spec, spec, -1, work)
    out_ref[:, 1] = inverse_signal(work, inverse, twiddle, last).astype(BF)


def inner_kernel(place_ref, weight_ref, query_ref, *refs):
    pieces = refs[:TP]
    inner_ref, gated_ref, keep_ref, send_ref = refs[TP:]
    core = place_ref[TP]
    total = jnp.zeros((ROWS, LOC), F32)
    for idx in range(TP):
        source = place_ref[idx]
        begin = pl.multiple_of(source * 512, 512)
        total = total + mm(weight_ref[:, pl.ds(begin, 512)], pieces[idx][...])
        for pair in range(2):
            slot = 2 * source + pair
            mine = pl.multiple_of(pair * 256 + core * 128, 128)
            other = pl.multiple_of(pair * 256 + (1 - core) * 128, 128)
            keep_ref[slot] = pieces[idx][pl.ds(mine, 128), :]
            send_ref[slot] = pieces[idx][pl.ds(other, 128), :]
    inner = total.astype(BF)
    inner_ref[...] = inner
    gated_ref[...] = (inner.astype(F32) * query_ref[...].astype(F32)).astype(BF)


def weight_kernel(place_ref, keep_ref, other_ref, mine_ref, sib_ref, own_ref, *outs):
    here = place_ref[0]
    for step in range(NX):
        want = lax.rem(here + step, NX)
        for z in range(NZ):
            slot = z * 4 + want
            part = lax.dot_general(
                keep_ref[slot], mine_ref[...], (((1,), (1,)), ((), ())), preferred_element_type=F32
            ) + lax.dot_general(
                other_ref[slot], sib_ref[...], (((1,), (1,)), ((), ())), preferred_element_type=F32
            )
            if step == 0:
                own_ref[z] = part
            else:
                outs[step - 1][z] = part.astype(BF)


def fold_kernel(place_ref, own_ref, one_ref, two_ref, three_ref, mine_ref, *outs):
    here = place_ref[1]
    for step in range(NZ):
        want = lax.rem(here + step, NZ)
        total = (
            own_ref[want]
            + one_ref[want].astype(F32)
            + two_ref[want].astype(F32)
            + three_ref[want].astype(F32)
        )
        if step == 0:
            mine_ref[...] = total
        else:
            outs[step - 1][...] = total.astype(BF)


def post_kernel(back_ref, inner_ref, conv_ref, key_ref, value_ref, post_ref, halo_ref, corr_ref):
    kv_grad = back_ref[:, 0].reshape(ROWS, LOC).astype(F32)
    grads = (
        inner_ref[...].astype(F32) * conv_ref[...].astype(F32),
        kv_grad * value_ref[...].astype(F32),
        kv_grad * key_ref[...].astype(F32),
    )
    lane = lax.broadcasted_iota(jnp.int32, (ROWS, FINE), 1)
    halo = jnp.zeros((ROWS, FINE), F32)
    for which in range(3):
        rounded = grads[which].astype(BF)
        post_ref[which] = rounded
        head = rounded[:, :FINE].astype(F32)
        if which:
            head = pltpu.roll(head, 8 * which, 1)
        halo = jnp.where((lane >= 8 * which) & (lane < 8 * which + 8), head, halo)
    halo_ref[...] = halo.astype(BF)
    corr_ref[...] = back_ref[:, 1].reshape(ROWS, LOC).astype(F32)


def feature_kernel(post_ref, halo_ref, taps_ref, out_ref):
    halo = halo_ref[...].astype(F32)
    for which in range(3):
        tail = halo if which == 0 else pltpu.roll(halo, FINE - 8 * which, 1)
        wide = jnp.concatenate([post_ref[which].astype(F32), tail], 1)
        taps = taps_ref[which]
        total = taps[:, 0:1] * wide[:, :LOC]
        for offset in range(1, 7):
            moved = pltpu.roll(wide, LOC + FINE - offset, 1)
            total = total + taps[:, offset : offset + 1] * moved[:, :LOC]
        out_ref[which] = total.astype(BF)


def call(kernel, outs, *args, scalars=0, scratch=(), name=None):
    specs = [pl.BlockSpec(memory_space=pltpu.SMEM)] * scalars
    specs += [pl.BlockSpec(memory_space=pltpu.VMEM)] * (len(args) - scalars)
    return pl.pallas_call(
        kernel,
        out_shape=[jax.ShapeDtypeStruct(shape, dtype) for shape, dtype in outs],
        in_specs=specs,
        out_specs=[pl.BlockSpec(memory_space=pltpu.VMEM)] * len(outs),
        scratch_shapes=list(scratch),
        compiler_params=pltpu.CompilerParams(vmem_limit_bytes=VMEM),
        name=name,
    )(*args)


def exchange(value):
    return lax.all_to_all(value, "ctx", split_axis=0, concat_axis=0, tiled=True)


def local(out_cotangent, query_rows, key_rows, value_rows, long_filter, short_filter, out_weight):
    ctx, tp = lax.axis_index("ctx"), lax.axis_index("tp")
    here_x, here_z, core = ctx // 2 % 4, ctx // 8, ctx % 2
    y, z_hi = tp // 2, tp % 2
    tables = [jnp.asarray(table) for table in make_tables()]

    far = lax.ppermute(out_cotangent, "tp", tp_shift(0, 1))
    pieces, sources = [out_cotangent, far], [tp, y * 2 + 1 - z_hi]
    for origin, flip in ((out_cotangent, 0), (far, 1)):
        for step in (1, 3, 2):
            pieces.append(lax.ppermute(origin, "tp", tp_shift(step, 0)))
            sources.append((y + 4 - step) % 4 * 2 + (z_hi + flip) % 2)
    place = jnp.stack(sources + [core]).astype(jnp.int32)

    (sent,) = call(
        prep_kernel, [((CTX, 2, CH, LOC), BF)], key_rows, value_rows, long_filter, name="prep"
    )
    weight_t = out_weight.T
    cols = exchange(sent)
    spec_shape = ((CH * KP, 2 * FINE), F32)
    conv_cols, kv_spec, fil_spec = call(
        conv_kernel,
        [((CTX, CH, LOC), BF), spec_shape, spec_shape],
        cols,
        *tables,
        scratch=[pltpu.VMEM(*spec_shape)],
        name="conv",
    )
    conv_out = exchange(conv_cols).reshape(ROWS, LOC)

    inner, gated, keep, send = call(
        inner_kernel,
        [((ROWS, LOC), BF), ((ROWS, LOC), BF), ((16, 128, LOC), BF), ((16, 128, LOC), BF)],
        place,
        weight_t,
        query_rows,
        *pieces,
        scalars=1,
        name="inner",
    )
    gated_cols = exchange(gated.reshape(CTX, CH, LOC))
    other = lax.ppermute(send, "ctx", ctx_shift(0, 0, 1))

    mixed = (query_rows.astype(F32) * conv_out.astype(F32)).astype(BF)
    mixed_sib = lax.ppermute(mixed, "ctx", ctx_shift(0, 0, 1))
    spot = jnp.stack([here_x, here_z]).astype(jnp.int32)
    part = (NZ, 128, 512)
    own, *to_x = call(
        weight_kernel,
        [(part, F32)] + [(part, BF)] * 3,
        spot,
        keep,
        other,
        mixed,
        mixed_sib,
        scalars=1,
        name="weight",
    )
    from_x = [
        lax.ppermute(to_x[step - 1], "ctx", ctx_shift(0, step, 0)) for step in (1, 2, 3)
    ]

    (back,) = call(
        grad_kernel,
        [((CTX, 2, CH, LOC), BF)],
        gated_cols,
        kv_spec,
        fil_spec,
        *tables,
        scratch=[pltpu.VMEM(*spec_shape), pltpu.VMEM(*spec_shape)],
        name="grad",
    )
    back = exchange(back)

    mine, *to_z = call(
        fold_kernel,
        [((128, 512), F32)] + [((128, 512), BF)] * 3,
        spot,
        own,
        *from_x,
        scalars=1,
        name="fold",
    )
    from_z = [
        lax.ppermute(to_z[step - 1], "ctx", ctx_shift(step, 0, 0)) for step in (1, 2, 3)
    ]
    out_weight_grad = mine + sum(value.astype(F32) for value in from_z)

    post, halo, filter_grad = call(
        post_kernel,
        [((3, ROWS, LOC), BF), ((ROWS, FINE), BF), ((ROWS, LOC), F32)],
        back,
        inner,
        conv_out,
        key_rows,
        value_rows,
        name="post",
    )
    halo = lax.ppermute(halo, "ctx", [(source, source - 1) for source in range(1, CTX)])
    (feature_grad,) = call(
        feature_kernel, [((3, ROWS, LOC), BF)], post, halo, short_filter, name="feature"
    )
    return (feature_grad, filter_grad, out_weight_grad)


def solution(mesh):
    return jax.shard_map(
        local,
        mesh=mesh,
        in_specs=(
            P("tp", "ctx"),
            P("tp", "ctx"),
            P("tp", "ctx"),
            P("tp", "ctx"),
            P("tp", "ctx"),
            P(None, "tp", None),
            P(None, "tp"),
        ),
        out_specs=(P(None, "tp", "ctx"), P("tp", "ctx"), P("ctx", "tp")),
        check_vma=False,
    )
```

```python
import math

import jax
import jax.numpy as jnp
import ml_dtypes
import numpy as np
from jax import lax
from jax.experimental import pallas as pl
from jax.experimental.pallas import tpu as pltpu
from jax.sharding import PartitionSpec as P

BF = jnp.bfloat16
F32 = jnp.float32
NX, NZ, NY = 4, 4, 4
CTX, TP = 32, 8
CH = 16
LOC = 256
ROWS = 512
KP = 72
FINE = 128
TOTAL = 16384
MIB = 1024 * 1024


def ctx_shift(dz, dx, dc):
    return [
        (z * 8 + x * 2 + c, (z + dz) % 4 * 8 + (x + dx) % 4 * 2 + (c + dc) % 2)
        for z in range(4)
        for x in range(4)
        for c in range(2)
    ]


def tp_shift(dy, dh):
    return [(y * 2 + h, (y + dy) % 4 * 2 + (h + dh) % 2) for y in range(4) for h in range(2)]


def split_np(table):
    high = table.astype(ml_dtypes.bfloat16)
    low = (table - high.astype(np.float64)).astype(ml_dtypes.bfloat16)
    return high, low


def make_tables():
    freq = np.arange(KP)[:, None]
    live = (freq <= 64).astype(np.float64)
    coarse = (2 * np.arange(32)[None, :] + np.arange(2)[:, None]).reshape(1, 64)
    angle = 2 * math.pi * ((freq * coarse) % 128) / 128
    first = np.concatenate([np.cos(angle) * live, -np.sin(angle) * live], 0)
    first = np.concatenate(split_np(first), 1)
    fine = np.arange(FINE)
    mid_angle = 2 * math.pi * ((fine[:, None] * fine[None, :]) % 128) / 128
    cos, sin = np.cos(mid_angle), np.sin(mid_angle)
    forward = np.stack(split_np(np.block([[cos, -sin], [sin, cos]])))
    inverse = np.stack(split_np(np.block([[cos, sin], [-sin, cos]])))
    tw_angle = 2 * math.pi * (freq * fine[None, :]) / TOTAL
    twiddle = np.stack([np.cos(tw_angle), np.sin(tw_angle)]).astype(np.float32)
    weight = np.where((freq == 0) | (freq == 64), 1.0, 2.0) * live / TOTAL
    last = np.concatenate([(np.cos(angle) * weight).T, (-np.sin(angle) * weight).T], 1)
    last = np.stack(split_np(last))
    return first, forward, inverse, twiddle, last


def halves(value):
    high = value.astype(BF)
    return high, (value - high.astype(F32)).astype(BF)


def mm(left, right):
    return jnp.dot(left, right, preferred_element_type=F32)


def mm_table(value, table_ref):
    high, low = halves(value)
    return mm(high, table_ref[0]) + mm(low, table_ref[0]) + mm(high, table_ref[1])


def forward_spectrum(block, first_ref, forward_ref, twiddle_ref, work_ref, spec_ref):
    chans = jnp.swapaxes(block.astype(F32), 0, 1).astype(BF)
    cos_tw, sin_tw = twiddle_ref[0], twiddle_ref[1]
    for pair in range(CH // 2):
        cols = []
        for chan in (2 * pair, 2 * pair + 1):
            both = jnp.concatenate([chans[chan, :, :FINE], chans[chan, :, FINE:]], 0)
            cols.append(jnp.concatenate([both, both], 0))
        coarse = mm(first_ref[...], jnp.concatenate(cols, 1))
        for which in range(2):
            real = coarse[:KP, which * FINE : (which + 1) * FINE]
            imag = coarse[KP:, which * FINE : (which + 1) * FINE]
            row = (2 * pair + which) * KP
            work_ref[row : row + KP, :FINE] = real * cos_tw + imag * sin_tw
            work_ref[row : row + KP, FINE:] = imag * cos_tw - real * sin_tw
    spec_ref[...] = mm_table(work_ref[...], forward_ref)


def inverse_signal(work_ref, inverse_ref, twiddle_ref, last_ref):
    work_ref[...] = mm_table(work_ref[...], inverse_ref)
    cos_tw, sin_tw = twiddle_ref[0], twiddle_ref[1]
    chans = []
    for pair in range(CH // 2):
        cols = []
        for chan in (2 * pair, 2 * pair + 1):
            real = work_ref[chan * KP : (chan + 1) * KP, :FINE]
            imag = work_ref[chan * KP : (chan + 1) * KP, FINE:]
            cols.append(
                jnp.concatenate(
                    [real * cos_tw - imag * sin_tw, imag * cos_tw + real * sin_tw], 0
                )
            )
        high, low = halves(jnp.concatenate(cols, 1))
        out = mm(last_ref[0], high) + mm(last_ref[0], low) + mm(last_ref[1], high)
        for which in range(2):
            mine = out[:, which * FINE : (which + 1) * FINE]
            chans.append(jnp.concatenate([mine[:32], mine[32:]], 1))
    return jnp.swapaxes(jnp.stack(chans, 0), 0, 1)


def times(left_ref, right_ref, sign_left, out_ref):
    lr, li = left_ref[:, :FINE], left_ref[:, FINE:]
    rr, ri = right_ref[:, :FINE], right_ref[:, FINE:]
    if sign_left > 0:
        out_ref[:, :FINE] = lr * rr - li * ri
        out_ref[:, FINE:] = lr * ri + li * rr
    else:
        out_ref[:, :FINE] = lr * rr + li * ri
        out_ref[:, FINE:] = lr * ri - li * rr


def prep_kernel(key_ref, value_ref, filter_ref, out_ref):
    kv = (key_ref[...].astype(F32) * value_ref[...].astype(F32)).astype(BF)
    out_ref[:, 0] = kv.reshape(CTX, CH, LOC)
    out_ref[:, 1] = filter_ref[...].astype(BF).reshape(CTX, CH, LOC)


def conv_kernel(in_ref, first, forward, inverse, twiddle, last, out_ref, kv_spec, fil_spec, work):
    forward_spectrum(in_ref[:, 0], first, forward, twiddle, work, kv_spec)
    forward_spectrum(in_ref[:, 1], first, forward, twiddle, work, fil_spec)
    times(fil_spec, kv_spec, 1, work)
    out_ref[...] = inverse_signal(work, inverse, twiddle, last).astype(BF)


def grad_kernel(
    in_ref, kv_spec, fil_spec, first, forward, inverse, twiddle, last, out_ref, spec, work
):
    forward_spectrum(in_ref[...], first, forward, twiddle, work, spec)
    times(fil_spec, spec, -1, work)
    out_ref[:, 0] = inverse_signal(work, inverse, twiddle, last).astype(BF)
    times(kv_spec, spec, -1, work)
    out_ref[:, 1] = inverse_signal(work, inverse, twiddle, last).astype(BF)


def staged(kernel, scalars, ins, outs):
    def body(*refs):
        at = scalars + ins
        far_in, far_out = refs[scalars:at], refs[at : at + outs]
        at += outs
        near_in, near_out = refs[at : at + ins], refs[at + ins : at + ins + outs]
        sems = refs[at + ins + outs]
        loads = [
            pltpu.make_async_copy(far_in[i], near_in[i], sems.at[i]) for i in range(ins)
        ]
        for load in loads:
            load.start()
        for load in loads:
            load.wait()
        kernel(*refs[:scalars], *near_in, *near_out, *refs[at + ins + outs + 1 :])
        stores = [
            pltpu.make_async_copy(near_out[i], far_out[i], sems.at[ins + i]) for i in range(outs)
        ]
        for store in stores:
            store.start()
        for store in stores:
            store.wait()

    return body


def call(kernel, outs, *args, scalars=0, scratch=(), name=None, us=3):
    arrays = args[scalars:]
    hbm = pl.BlockSpec(memory_space=pltpu.HBM)
    specs = [pl.BlockSpec(memory_space=pltpu.SMEM)] * scalars + [hbm] * len(arrays)
    return pl.pallas_call(
        staged(kernel, scalars, len(arrays), len(outs)),
        out_shape=[jax.ShapeDtypeStruct(shape, dtype) for shape, dtype in outs],
        in_specs=specs,
        out_specs=[hbm] * len(outs),
        scratch_shapes=[pltpu.VMEM(arg.shape, arg.dtype) for arg in arrays]
        + [pltpu.VMEM(shape, dtype) for shape, dtype in outs]
        + [pltpu.SemaphoreType.DMA((len(arrays) + len(outs),))]
        + list(scratch),
        compiler_params=pltpu.CompilerParams(vmem_limit_bytes=60 * MIB),
        cost_estimate=pl.CostEstimate(
            flops=us * 10**9, bytes_accessed=us * 3 * 10**6, transcendentals=0
        ),
        name=name,
    )(*args)


def inner_kernel(place_ref, weight_hbm, query_hbm, *refs):
    pieces_hbm, refs = refs[:TP], refs[TP:]
    inner_hbm, gated_hbm, keep_hbm, send_hbm = refs[:4]
    weight, pieces, query, inner_ref, gated_ref, load_sem, query_sem, store_sem = refs[4:]
    core = place_ref[TP]
    loads = []
    for idx in range(TP):
        begin = pl.multiple_of(place_ref[idx] * 512, 512)
        loads.append(
            [
                pltpu.make_async_copy(
                    weight_hbm.at[:, pl.ds(begin, 512)], weight.at[idx], load_sem.at[2 * idx]
                ),
                pltpu.make_async_copy(
                    pieces_hbm[idx], pieces.at[idx], load_sem.at[2 * idx + 1]
                ),
            ]
        )
        for load in loads[-1]:
            load.start()
    query_load = pltpu.make_async_copy(query_hbm, query, query_sem)
    query_load.start()
    total = jnp.zeros((ROWS, LOC), F32)
    stores = []
    for idx in range(TP):
        for load in loads[idx]:
            load.wait()
        total = total + mm(weight[idx], pieces[idx])
        for pair in range(2):
            slot = 2 * place_ref[idx] + pair
            mine = pl.multiple_of(pair * 256 + core * 128, 128)
            other = pl.multiple_of(pair * 256 + (1 - core) * 128, 128)
            for where, begin, kind in ((keep_hbm, mine, 0), (send_hbm, other, 1)):
                stores.append(
                    pltpu.make_async_copy(
                        pieces.at[idx, pl.ds(begin, 128)],
                        where.at[slot],
                        store_sem.at[4 * idx + 2 * pair + kind],
                    )
                )
                stores[-1].start()
    query_load.wait()
    inner = total.astype(BF)
    inner_ref[...] = inner
    gated_ref[...] = (inner.astype(F32) * query[...].astype(F32)).astype(BF)
    for near, far, sem in ((inner_ref, inner_hbm, 4 * TP), (gated_ref, gated_hbm, 4 * TP + 1)):
        stores.append(pltpu.make_async_copy(near, far, store_sem.at[sem]))
        stores[-1].start()
    for store in stores:
        store.wait()


def inner_call(place, weight_t, query, pieces):
    hbm = pl.BlockSpec(memory_space=pltpu.HBM)
    shapes = [(ROWS, LOC), (ROWS, LOC), (16, 128, LOC), (16, 128, LOC)]
    return pl.pallas_call(
        inner_kernel,
        out_shape=[jax.ShapeDtypeStruct(shape, BF) for shape in shapes],
        in_specs=[pl.BlockSpec(memory_space=pltpu.SMEM)] + [hbm] * (TP + 2),
        out_specs=[hbm] * 4,
        scratch_shapes=[
            pltpu.VMEM((TP, ROWS, 512), BF),
            pltpu.VMEM((TP, 512, LOC), BF),
            pltpu.VMEM((ROWS, LOC), BF),
            pltpu.VMEM((ROWS, LOC), BF),
            pltpu.VMEM((ROWS, LOC), BF),
            pltpu.SemaphoreType.DMA((2 * TP,)),
            pltpu.SemaphoreType.DMA,
            pltpu.SemaphoreType.DMA((4 * TP + 2,)),
        ],
        compiler_params=pltpu.CompilerParams(vmem_limit_bytes=60 * MIB),
        cost_estimate=pl.CostEstimate(
            flops=30 * 10**9, bytes_accessed=90 * 10**6, transcendentals=0
        ),
        name="inner",
    )(place, weight_t, query, *pieces)


def weight_kernel(place_ref, keep_ref, other_ref, mine_ref, sib_ref, own_ref, *outs):
    here = place_ref[0]
    for step in range(NX):
        want = lax.rem(here + step, NX)
        rows = jnp.concatenate(
            [
                jnp.concatenate([keep_ref[z * 4 + want], other_ref[z * 4 + want]], 1)
                for z in range(NZ)
            ],
            0,
        )
        cols = jnp.concatenate([mine_ref[...], sib_ref[...]], 1)
        part = lax.dot_general(
            rows, cols, (((1,), (1,)), ((), ())), preferred_element_type=F32
        ).reshape(NZ, 128, 512)
        if step == 0:
            own_ref[...] = part
        else:
            outs[step - 1][...] = part.astype(BF)


def fold_kernel(place_ref, own_ref, one_ref, two_ref, three_ref, mine_ref, *outs):
    here = place_ref[1]
    for step in range(NZ):
        want = lax.rem(here + step, NZ)
        total = (
            own_ref[want]
            + one_ref[want].astype(F32)
            + two_ref[want].astype(F32)
            + three_ref[want].astype(F32)
        )
        if step == 0:
            mine_ref[...] = total
        else:
            outs[step - 1][...] = total.astype(BF)


def post_kernel(back_ref, inner_ref, conv_ref, key_ref, value_ref, post_ref, halo_ref, corr_ref):
    kv_grad = back_ref[:, 0].reshape(ROWS, LOC).astype(F32)
    grads = (
        inner_ref[...].astype(F32) * conv_ref[...].astype(F32),
        kv_grad * value_ref[...].astype(F32),
        kv_grad * key_ref[...].astype(F32),
    )
    lane = lax.broadcasted_iota(jnp.int32, (ROWS, FINE), 1)
    halo = jnp.zeros((ROWS, FINE), F32)
    for which in range(3):
        rounded = grads[which].astype(BF)
        post_ref[which] = rounded
        head = rounded[:, :FINE].astype(F32)
        if which:
            head = pltpu.roll(head, 8 * which, 1)
        halo = jnp.where((lane >= 8 * which) & (lane < 8 * which + 8), head, halo)
    halo_ref[...] = halo.astype(BF)
    corr_ref[...] = back_ref[:, 1].reshape(ROWS, LOC).astype(F32)


def feature_kernel(post_ref, halo_ref, taps_ref, out_ref):
    halo = halo_ref[...].astype(F32)
    for which in range(3):
        tail = halo if which == 0 else pltpu.roll(halo, FINE - 8 * which, 1)
        wide = jnp.concatenate([post_ref[which].astype(F32), tail], 1)
        taps = taps_ref[which]
        total = taps[:, 0:1] * wide[:, :LOC]
        for offset in range(1, 7):
            moved = pltpu.roll(wide, LOC + FINE - offset, 1)
            total = total + taps[:, offset : offset + 1] * moved[:, :LOC]
        out_ref[which] = total.astype(BF)


def exchange(value):
    return lax.all_to_all(value, "ctx", split_axis=0, concat_axis=0, tiled=True)


def local(out_cotangent, query_rows, key_rows, value_rows, long_filter, short_filter, out_weight):
    ctx, tp = lax.axis_index("ctx"), lax.axis_index("tp")
    here_x, here_z, core = ctx // 2 % 4, ctx // 8, ctx % 2
    y, z_hi = tp // 2, tp % 2
    tables = [jnp.asarray(table) for table in make_tables()]

    far = lax.ppermute(out_cotangent, "tp", tp_shift(0, 1))
    near = [lax.ppermute(out_cotangent, "tp", tp_shift(step, 0)) for step in (1, 3, 2)]
    (sent,) = call(
        prep_kernel, [((CTX, 2, CH, LOC), BF)], key_rows, value_rows, long_filter, name="prep"
    )
    sent, far, *near = lax.optimization_barrier((sent, far, *near))
    pieces = [out_cotangent, far] + near
    pieces += [lax.ppermute(far, "tp", tp_shift(step, 0)) for step in (1, 3, 2)]
    sources = [tp, y * 2 + 1 - z_hi]
    for flip in (0, 1):
        for step in (1, 3, 2):
            sources.append((y + 4 - step) % 4 * 2 + (z_hi + flip) % 2)
    place = jnp.stack(sources + [core]).astype(jnp.int32)

    cols = exchange(sent)
    weight_t = out_weight.T
    spec_shape = ((CH * KP, 2 * FINE), F32)
    conv_cols, kv_spec, fil_spec = call(
        conv_kernel,
        [((CTX, CH, LOC), BF), spec_shape, spec_shape],
        cols,
        *tables,
        scratch=[pltpu.VMEM(*spec_shape)],
        name="conv",
        us=30,
    )
    conv_cols, place = lax.optimization_barrier((conv_cols, place))
    conv_out = exchange(conv_cols)
    inner, gated, keep, send = inner_call(place, weight_t, query_rows, pieces)
    conv_out, gated, send = lax.optimization_barrier((conv_out, gated, send))
    conv_out = conv_out.reshape(ROWS, LOC)
    gated_cols = exchange(gated.reshape(CTX, CH, LOC))
    other = lax.ppermute(send, "ctx", ctx_shift(0, 0, 1))
    mixed = (query_rows.astype(F32) * conv_out.astype(F32)).astype(BF)
    mixed_sib = lax.ppermute(mixed, "ctx", ctx_shift(0, 0, 1))
    spot = jnp.stack([here_x, here_z]).astype(jnp.int32)
    part = (NZ, 128, 512)
    own, *to_x = call(
        weight_kernel,
        [(part, F32)] + [(part, BF)] * 3,
        spot,
        keep,
        other,
        mixed,
        mixed_sib,
        scalars=1,
        name="weight",
    )
    from_x = [
        lax.ppermute(to_x[step - 1], "ctx", ctx_shift(0, step, 0)) for step in (1, 2, 3)
    ]

    gated_cols, own = lax.optimization_barrier((gated_cols, own))
    (back,) = call(
        grad_kernel,
        [((CTX, 2, CH, LOC), BF)],
        gated_cols,
        kv_spec,
        fil_spec,
        *tables,
        scratch=[pltpu.VMEM(*spec_shape), pltpu.VMEM(*spec_shape)],
        name="grad",
        us=30,
    )
    back = exchange(back)

    mine, *to_z = call(
        fold_kernel,
        [((128, 512), F32)] + [((128, 512), BF)] * 3,
        spot,
        own,
        *from_x,
        scalars=1,
        name="fold",
        us=30,
    )
    from_z = [
        lax.ppermute(to_z[step - 1], "ctx", ctx_shift(step, 0, 0)) for step in (1, 2, 3)
    ]
    back, mine = lax.optimization_barrier((back, mine))
    post, halo, filter_grad = call(
        post_kernel,
        [((3, ROWS, LOC), BF), ((ROWS, FINE), BF), ((ROWS, LOC), F32)],
        back,
        inner,
        conv_out,
        key_rows,
        value_rows,
        name="post",
    )
    halo = lax.ppermute(halo, "ctx", [(source, source - 1) for source in range(1, CTX)])
    (feature_grad,) = call(
        feature_kernel, [((3, ROWS, LOC), BF)], post, halo, short_filter, name="feature"
    )
    mine, feature_grad = lax.optimization_barrier((mine, feature_grad))
    out_weight_grad = mine + sum(value.astype(F32) for value in from_z)

    return (feature_grad, filter_grad, out_weight_grad)


def solution(mesh):
    return jax.shard_map(
        local,
        mesh=mesh,
        in_specs=(
            P("tp", "ctx"),
            P("tp", "ctx"),
            P("tp", "ctx"),
            P("tp", "ctx"),
            P("tp", "ctx"),
            P(None, "tp", None),
            P(None, "tp"),
        ),
        out_specs=(P(None, "tp", "ctx"), P("tp", "ctx"), P("ctx", "tp")),
        check_vma=False,
    )
```

```python
import math

import jax
import jax.numpy as jnp
import ml_dtypes
import numpy as np
from jax import lax
from jax.experimental import pallas as pl
from jax.experimental.pallas import tpu as pltpu
from jax.sharding import PartitionSpec as P

BF = jnp.bfloat16
F32 = jnp.float32
NX, NZ, NY = 4, 4, 4
CTX, TP = 32, 8
CH = 16
LOC = 256
ROWS = 512
KP = 72
FINE = 128
TOTAL = 16384
MIB = 1024 * 1024


def ctx_shift(dz, dx, dc):
    return [
        (z * 8 + x * 2 + c, (z + dz) % 4 * 8 + (x + dx) % 4 * 2 + (c + dc) % 2)
        for z in range(4)
        for x in range(4)
        for c in range(2)
    ]


def tp_shift(dy, dh):
    return [(y * 2 + h, (y + dy) % 4 * 2 + (h + dh) % 2) for y in range(4) for h in range(2)]


def split_np(table):
    high = table.astype(ml_dtypes.bfloat16)
    low = (table - high.astype(np.float64)).astype(ml_dtypes.bfloat16)
    return high, low


def make_tables():
    freq = np.arange(KP)[:, None]
    live = (freq <= 64).astype(np.float64)
    coarse = (2 * np.arange(32)[None, :] + np.arange(2)[:, None]).reshape(1, 64)
    angle = 2 * math.pi * ((freq * coarse) % 128) / 128
    first = np.concatenate([np.cos(angle) * live, -np.sin(angle) * live], 0)
    first = np.concatenate(split_np(first), 1)
    fine = np.arange(FINE)
    mid_angle = 2 * math.pi * ((fine[:, None] * fine[None, :]) % 128) / 128
    cos, sin = np.cos(mid_angle), np.sin(mid_angle)
    forward = np.stack(split_np(np.block([[cos, -sin], [sin, cos]])))
    inverse = np.stack(split_np(np.block([[cos, sin], [-sin, cos]])))
    tw_angle = 2 * math.pi * (freq * fine[None, :]) / TOTAL
    twiddle = np.stack([np.cos(tw_angle), np.sin(tw_angle)]).astype(np.float32)
    weight = np.where((freq == 0) | (freq == 64), 1.0, 2.0) * live / TOTAL
    last = np.concatenate([(np.cos(angle) * weight).T, (-np.sin(angle) * weight).T], 1)
    last = np.stack(split_np(last))
    return first, forward, inverse, twiddle, last


def halves(value):
    high = value.astype(BF)
    return high, (value - high.astype(F32)).astype(BF)


def mm(left, right):
    return jnp.dot(left, right, preferred_element_type=F32)


def mm_table(value, table_ref):
    high, low = halves(value)
    return mm(high, table_ref[0]) + mm(low, table_ref[0]) + mm(high, table_ref[1])


def forward_spectrum(block, first_ref, forward_ref, twiddle_ref, work_ref, spec_ref):
    chans = jnp.swapaxes(block.astype(F32), 0, 1).astype(BF)
    cos_tw, sin_tw = twiddle_ref[0], twiddle_ref[1]
    for pair in range(CH // 2):
        cols = []
        for chan in (2 * pair, 2 * pair + 1):
            both = jnp.concatenate([chans[chan, :, :FINE], chans[chan, :, FINE:]], 0)
            cols.append(jnp.concatenate([both, both], 0))
        coarse = mm(first_ref[...], jnp.concatenate(cols, 1))
        for which in range(2):
            real = coarse[:KP, which * FINE : (which + 1) * FINE]
            imag = coarse[KP:, which * FINE : (which + 1) * FINE]
            row = (2 * pair + which) * KP
            work_ref[row : row + KP, :FINE] = real * cos_tw + imag * sin_tw
            work_ref[row : row + KP, FINE:] = imag * cos_tw - real * sin_tw
    spec_ref[...] = mm_table(work_ref[...], forward_ref)


def inverse_signal(work_ref, inverse_ref, twiddle_ref, last_ref):
    work_ref[...] = mm_table(work_ref[...], inverse_ref)
    cos_tw, sin_tw = twiddle_ref[0], twiddle_ref[1]
    chans = []
    for pair in range(CH // 2):
        cols = []
        for chan in (2 * pair, 2 * pair + 1):
            real = work_ref[chan * KP : (chan + 1) * KP, :FINE]
            imag = work_ref[chan * KP : (chan + 1) * KP, FINE:]
            cols.append(
                jnp.concatenate(
                    [real * cos_tw - imag * sin_tw, imag * cos_tw + real * sin_tw], 0
                )
            )
        high, low = halves(jnp.concatenate(cols, 1))
        out = mm(last_ref[0], high) + mm(last_ref[0], low) + mm(last_ref[1], high)
        for which in range(2):
            mine = out[:, which * FINE : (which + 1) * FINE]
            chans.append(jnp.concatenate([mine[:32], mine[32:]], 1))
    return jnp.swapaxes(jnp.stack(chans, 0), 0, 1)


def times(left_ref, right_ref, sign_left, out_ref):
    lr, li = left_ref[:, :FINE], left_ref[:, FINE:]
    rr, ri = right_ref[:, :FINE], right_ref[:, FINE:]
    if sign_left > 0:
        out_ref[:, :FINE] = lr * rr - li * ri
        out_ref[:, FINE:] = lr * ri + li * rr
    else:
        out_ref[:, :FINE] = lr * rr + li * ri
        out_ref[:, FINE:] = lr * ri - li * rr


def prep_kernel(key_ref, value_ref, filter_ref, out_ref):
    kv = (key_ref[...].astype(F32) * value_ref[...].astype(F32)).astype(BF)
    out_ref[:, 0] = kv.reshape(CTX, CH, LOC)
    out_ref[:, 1] = filter_ref[...].astype(BF).reshape(CTX, CH, LOC)


def conv_kernel(in_ref, first, forward, inverse, twiddle, last, out_ref, kv_spec, fil_spec, work):
    forward_spectrum(in_ref[:, 0], first, forward, twiddle, work, kv_spec)
    forward_spectrum(in_ref[:, 1], first, forward, twiddle, work, fil_spec)
    times(fil_spec, kv_spec, 1, work)
    out_ref[...] = inverse_signal(work, inverse, twiddle, last).astype(BF)


def grad_kernel(
    in_ref, kv_spec, fil_spec, first, forward, inverse, twiddle, last, out_ref, spec, work
):
    forward_spectrum(in_ref[...], first, forward, twiddle, work, spec)
    times(fil_spec, spec, -1, work)
    out_ref[:, 0] = inverse_signal(work, inverse, twiddle, last).astype(BF)
    times(kv_spec, spec, -1, work)
    out_ref[:, 1] = inverse_signal(work, inverse, twiddle, last).astype(BF)


def staged(kernel, scalars, ins, outs):
    def body(*refs):
        at = scalars + ins
        far_in, far_out = refs[scalars:at], refs[at : at + outs]
        at += outs
        near_in, near_out = refs[at : at + ins], refs[at + ins : at + ins + outs]
        sems = refs[at + ins + outs]
        loads = [
            pltpu.make_async_copy(far_in[i], near_in[i], sems.at[i]) for i in range(ins)
        ]
        for load in loads:
            load.start()
        for load in loads:
            load.wait()
        kernel(*refs[:scalars], *near_in, *near_out, *refs[at + ins + outs + 1 :])
        stores = [
            pltpu.make_async_copy(near_out[i], far_out[i], sems.at[ins + i]) for i in range(outs)
        ]
        for store in stores:
            store.start()
        for store in stores:
            store.wait()

    return body


def call(kernel, outs, *args, scalars=0, scratch=(), name=None, us=3):
    arrays = args[scalars:]
    hbm = pl.BlockSpec(memory_space=pltpu.HBM)
    specs = [pl.BlockSpec(memory_space=pltpu.SMEM)] * scalars + [hbm] * len(arrays)
    return pl.pallas_call(
        staged(kernel, scalars, len(arrays), len(outs)),
        out_shape=[jax.ShapeDtypeStruct(shape, dtype) for shape, dtype in outs],
        in_specs=specs,
        out_specs=[hbm] * len(outs),
        scratch_shapes=[pltpu.VMEM(arg.shape, arg.dtype) for arg in arrays]
        + [pltpu.VMEM(shape, dtype) for shape, dtype in outs]
        + [pltpu.SemaphoreType.DMA((len(arrays) + len(outs),))]
        + list(scratch),
        compiler_params=pltpu.CompilerParams(vmem_limit_bytes=60 * MIB),
        cost_estimate=pl.CostEstimate(
            flops=us * 10**9, bytes_accessed=us * 3 * 10**6, transcendentals=0
        ),
        name=name,
    )(*args)


def inner_kernel(place_ref, weight_hbm, query_hbm, *refs):
    pieces_hbm, refs = refs[:TP], refs[TP:]
    inner_hbm, gated_hbm, keep_hbm, send_hbm = refs[:4]
    weight, pieces, query, inner_ref, gated_ref, load_sem, query_sem, store_sem = refs[4:]
    core = place_ref[TP]
    loads = []
    for idx in range(TP):
        begin = pl.multiple_of(place_ref[idx] * 512, 512)
        loads.append(
            [
                pltpu.make_async_copy(
                    weight_hbm.at[:, pl.ds(begin, 512)], weight.at[idx], load_sem.at[2 * idx]
                ),
                pltpu.make_async_copy(
                    pieces_hbm[idx], pieces.at[idx], load_sem.at[2 * idx + 1]
                ),
            ]
        )
        for load in loads[-1]:
            load.start()
    query_load = pltpu.make_async_copy(query_hbm, query, query_sem)
    query_load.start()
    total = jnp.zeros((ROWS, LOC), F32)
    stores = []
    for idx in range(TP):
        for load in loads[idx]:
            load.wait()
        total = total + mm(weight[idx], pieces[idx])
        for pair in range(2):
            slot = 2 * place_ref[idx] + pair
            mine = pl.multiple_of(pair * 256 + core * 128, 128)
            other = pl.multiple_of(pair * 256 + (1 - core) * 128, 128)
            for where, begin, kind in ((keep_hbm, mine, 0), (send_hbm, other, 1)):
                stores.append(
                    pltpu.make_async_copy(
                        pieces.at[idx, pl.ds(begin, 128)],
                        where.at[slot],
                        store_sem.at[4 * idx + 2 * pair + kind],
                    )
                )
                stores[-1].start()
    query_load.wait()
    inner = total.astype(BF)
    inner_ref[...] = inner
    gated_ref[...] = (inner.astype(F32) * query[...].astype(F32)).astype(BF)
    for near, far, sem in ((inner_ref, inner_hbm, 4 * TP), (gated_ref, gated_hbm, 4 * TP + 1)):
        stores.append(pltpu.make_async_copy(near, far, store_sem.at[sem]))
        stores[-1].start()
    for store in stores:
        store.wait()


def inner_call(place, weight_t, query, pieces):
    hbm = pl.BlockSpec(memory_space=pltpu.HBM)
    shapes = [(ROWS, LOC), (ROWS, LOC), (16, 128, LOC), (16, 128, LOC)]
    return pl.pallas_call(
        inner_kernel,
        out_shape=[jax.ShapeDtypeStruct(shape, BF) for shape in shapes],
        in_specs=[pl.BlockSpec(memory_space=pltpu.SMEM)] + [hbm] * (TP + 2),
        out_specs=[hbm] * 4,
        scratch_shapes=[
            pltpu.VMEM((TP, ROWS, 512), BF),
            pltpu.VMEM((TP, 512, LOC), BF),
            pltpu.VMEM((ROWS, LOC), BF),
            pltpu.VMEM((ROWS, LOC), BF),
            pltpu.VMEM((ROWS, LOC), BF),
            pltpu.SemaphoreType.DMA((2 * TP,)),
            pltpu.SemaphoreType.DMA,
            pltpu.SemaphoreType.DMA((4 * TP + 2,)),
        ],
        compiler_params=pltpu.CompilerParams(vmem_limit_bytes=60 * MIB),
        cost_estimate=pl.CostEstimate(
            flops=30 * 10**9, bytes_accessed=90 * 10**6, transcendentals=0
        ),
        name="inner",
    )(place, weight_t, query, *pieces)


def weight_kernel(place_ref, keep_ref, other_ref, mine_ref, sib_ref, own_ref, *outs):
    here = place_ref[0]
    for step in range(NX):
        want = lax.rem(here + step, NX)
        rows = jnp.concatenate(
            [
                jnp.concatenate([keep_ref[z * 4 + want], other_ref[z * 4 + want]], 1)
                for z in range(NZ)
            ],
            0,
        )
        cols = jnp.concatenate([mine_ref[...], sib_ref[...]], 1)
        part = lax.dot_general(
            rows, cols, (((1,), (1,)), ((), ())), preferred_element_type=F32
        ).reshape(NZ, 128, 512)
        if step == 0:
            own_ref[...] = part
        else:
            outs[step - 1][...] = part.astype(BF)


def fold_kernel(place_ref, own_ref, one_ref, two_ref, three_ref, mine_ref, *outs):
    here = place_ref[1]
    for step in range(NZ):
        want = lax.rem(here + step, NZ)
        total = (
            own_ref[want]
            + one_ref[want].astype(F32)
            + two_ref[want].astype(F32)
            + three_ref[want].astype(F32)
        )
        if step == 0:
            mine_ref[...] = total
        else:
            outs[step - 1][...] = total.astype(BF)


def post_kernel(back_ref, inner_ref, conv_ref, key_ref, value_ref, post_ref, halo_ref, corr_ref):
    kv_grad = back_ref[:, 0].reshape(ROWS, LOC).astype(F32)
    grads = (
        inner_ref[...].astype(F32) * conv_ref[...].astype(F32),
        kv_grad * value_ref[...].astype(F32),
        kv_grad * key_ref[...].astype(F32),
    )
    lane = lax.broadcasted_iota(jnp.int32, (ROWS, FINE), 1)
    halo = jnp.zeros((ROWS, FINE), F32)
    for which in range(3):
        rounded = grads[which].astype(BF)
        post_ref[which] = rounded
        head = rounded[:, :FINE].astype(F32)
        if which:
            head = pltpu.roll(head, 8 * which, 1)
        halo = jnp.where((lane >= 8 * which) & (lane < 8 * which + 8), head, halo)
    halo_ref[...] = halo.astype(BF)
    corr_ref[...] = back_ref[:, 1].reshape(ROWS, LOC).astype(F32)


def feature_kernel(post_ref, halo_ref, taps_ref, out_ref):
    halo = halo_ref[...].astype(F32)
    for which in range(3):
        tail = halo if which == 0 else pltpu.roll(halo, FINE - 8 * which, 1)
        wide = jnp.concatenate([post_ref[which].astype(F32), tail], 1)
        taps = jnp.concatenate([taps_ref[which], jnp.zeros((1, ROWS), F32)], 0).T
        total = taps[:, 0:1] * wide[:, :LOC]
        for offset in range(1, 7):
            moved = pltpu.roll(wide, LOC + FINE - offset, 1)
            total = total + taps[:, offset : offset + 1] * moved[:, :LOC]
        out_ref[which] = total.astype(BF)


def exchange(value):
    return lax.all_to_all(value, "ctx", split_axis=0, concat_axis=0, tiled=True)


def local(out_cotangent, query_rows, key_rows, value_rows, long_filter, short_filter, out_weight):
    ctx, tp = lax.axis_index("ctx"), lax.axis_index("tp")
    here_x, here_z, core = ctx // 2 % 4, ctx // 8, ctx % 2
    y, z_hi = tp // 2, tp % 2
    tables = [jnp.asarray(table) for table in make_tables()]

    far = lax.ppermute(out_cotangent, "tp", tp_shift(0, 1))
    near = [lax.ppermute(out_cotangent, "tp", tp_shift(step, 0)) for step in (1, 3, 2)]
    (sent,) = call(
        prep_kernel, [((CTX, 2, CH, LOC), BF)], key_rows, value_rows, long_filter, name="prep"
    )
    sent, far, *near = lax.optimization_barrier((sent, far, *near))
    pieces = [out_cotangent, far] + near
    pieces += [lax.ppermute(far, "tp", tp_shift(step, 0)) for step in (1, 3, 2)]
    sources = [tp, y * 2 + 1 - z_hi]
    for flip in (0, 1):
        for step in (1, 3, 2):
            sources.append((y + 4 - step) % 4 * 2 + (z_hi + flip) % 2)
    place = jnp.stack(sources + [core]).astype(jnp.int32)

    cols = exchange(sent)
    weight_t = out_weight.T
    spec_shape = ((CH * KP, 2 * FINE), F32)
    conv_cols, kv_spec, fil_spec = call(
        conv_kernel,
        [((CTX, CH, LOC), BF), spec_shape, spec_shape],
        cols,
        *tables,
        scratch=[pltpu.VMEM(*spec_shape)],
        name="conv",
        us=30,
    )
    conv_cols, place = lax.optimization_barrier((conv_cols, place))
    conv_out = exchange(conv_cols)
    inner, gated, keep, send = inner_call(place, weight_t, query_rows, pieces)
    conv_out, gated, send = lax.optimization_barrier((conv_out, gated, send))
    conv_out = conv_out.reshape(ROWS, LOC)
    gated_cols = exchange(gated.reshape(CTX, CH, LOC))
    other = lax.ppermute(send, "ctx", ctx_shift(0, 0, 1))
    mixed = (query_rows.astype(F32) * conv_out.astype(F32)).astype(BF)
    mixed_sib = lax.ppermute(mixed, "ctx", ctx_shift(0, 0, 1))
    spot = jnp.stack([here_x, here_z]).astype(jnp.int32)
    part = (NZ, 128, 512)
    own, *to_x = call(
        weight_kernel,
        [(part, F32)] + [(part, BF)] * 3,
        spot,
        keep,
        other,
        mixed,
        mixed_sib,
        scalars=1,
        name="weight",
    )
    from_x = [
        lax.ppermute(to_x[step - 1], "ctx", ctx_shift(0, step, 0)) for step in (1, 2, 3)
    ]

    gated_cols, own = lax.optimization_barrier((gated_cols, own))
    (back,) = call(
        grad_kernel,
        [((CTX, 2, CH, LOC), BF)],
        gated_cols,
        kv_spec,
        fil_spec,
        *tables,
        scratch=[pltpu.VMEM(*spec_shape), pltpu.VMEM(*spec_shape)],
        name="grad",
        us=5,
    )
    back = exchange(back)

    mine, *to_z = call(
        fold_kernel,
        [((128, 512), F32)] + [((128, 512), BF)] * 3,
        spot,
        own,
        *from_x,
        scalars=1,
        name="fold",
        us=30,
    )
    from_z = [
        lax.ppermute(to_z[step - 1], "ctx", ctx_shift(step, 0, 0)) for step in (1, 2, 3)
    ]
    back, mine = lax.optimization_barrier((back, mine))
    post, halo, filter_grad = call(
        post_kernel,
        [((3, ROWS, LOC), BF), ((ROWS, FINE), BF), ((ROWS, LOC), F32)],
        back,
        inner,
        conv_out,
        key_rows,
        value_rows,
        name="post",
    )
    halo = lax.ppermute(halo, "ctx", [(source, source - 1) for source in range(1, CTX)])
    (feature_grad,) = call(
        feature_kernel, [((3, ROWS, LOC), BF)], post, halo, short_filter.transpose(0, 2, 1), name="feature"
    )
    mine, feature_grad = lax.optimization_barrier((mine, feature_grad))
    out_weight_grad = mine + sum(value.astype(F32) for value in from_z)

    return (feature_grad, filter_grad, out_weight_grad)


def solution(mesh):
    return jax.shard_map(
        local,
        mesh=mesh,
        in_specs=(
            P("tp", "ctx"),
            P("tp", "ctx"),
            P("tp", "ctx"),
            P("tp", "ctx"),
            P("tp", "ctx"),
            P(None, "tp", None),
            P(None, "tp"),
        ),
        out_specs=(P(None, "tp", "ctx"), P("tp", "ctx"), P("ctx", "tp")),
        check_vma=False,
    )
```

```python
import math

import jax
import jax.numpy as jnp
import ml_dtypes
import numpy as np
from jax import lax
from jax.experimental import pallas as pl
from jax.experimental.pallas import tpu as pltpu
from jax.sharding import PartitionSpec as P

BF = jnp.bfloat16
F32 = jnp.float32
NX, NZ, NY = 4, 4, 4
CTX, TP = 32, 8
CH = 16
LOC = 256
ROWS = 512
KP = 72
FINE = 128
TOTAL = 16384
MIB = 1024 * 1024


def ctx_shift(dz, dx, dc):
    return [
        (z * 8 + x * 2 + c, (z + dz) % 4 * 8 + (x + dx) % 4 * 2 + (c + dc) % 2)
        for z in range(4)
        for x in range(4)
        for c in range(2)
    ]


def tp_shift(dy, dh):
    return [(y * 2 + h, (y + dy) % 4 * 2 + (h + dh) % 2) for y in range(4) for h in range(2)]


def split_np(table):
    high = table.astype(ml_dtypes.bfloat16)
    low = (table - high.astype(np.float64)).astype(ml_dtypes.bfloat16)
    return high, low


def make_tables():
    freq = np.arange(KP)[:, None]
    live = (freq <= 64).astype(np.float64)
    coarse = (2 * np.arange(32)[None, :] + np.arange(2)[:, None]).reshape(1, 64)
    angle = 2 * math.pi * ((freq * coarse) % 128) / 128
    first = np.concatenate([np.cos(angle) * live, -np.sin(angle) * live], 0)
    first = np.concatenate(split_np(first), 1)
    fine = np.arange(FINE)
    mid_angle = 2 * math.pi * ((fine[:, None] * fine[None, :]) % 128) / 128
    cos, sin = np.cos(mid_angle), np.sin(mid_angle)
    forward = np.stack(split_np(np.block([[cos, -sin], [sin, cos]])))
    inverse = np.stack(split_np(np.block([[cos, sin], [-sin, cos]])))
    tw_angle = 2 * math.pi * (freq * fine[None, :]) / TOTAL
    twiddle = np.stack([np.cos(tw_angle), np.sin(tw_angle)]).astype(np.float32)
    weight = np.where((freq == 0) | (freq == 64), 1.0, 2.0) * live / TOTAL
    last = np.concatenate([(np.cos(angle) * weight).T, (-np.sin(angle) * weight).T], 1)
    last = np.stack(split_np(last))
    return first, forward, inverse, twiddle, last


def halves(value):
    high = value.astype(BF)
    return high, (value - high.astype(F32)).astype(BF)


def mm(left, right):
    return jnp.dot(left, right, preferred_element_type=F32)


def mm_table(value, table_ref):
    high, low = halves(value)
    return mm(high, table_ref[0]) + mm(low, table_ref[0]) + mm(high, table_ref[1])


def forward_spectrum(block, first_ref, forward_ref, twiddle_ref, work_ref, spec_ref):
    chans = jnp.swapaxes(block.astype(F32), 0, 1).astype(BF)
    cos_tw, sin_tw = twiddle_ref[0], twiddle_ref[1]
    for pair in range(CH // 2):
        cols = []
        for chan in (2 * pair, 2 * pair + 1):
            both = jnp.concatenate([chans[chan, :, :FINE], chans[chan, :, FINE:]], 0)
            cols.append(jnp.concatenate([both, both], 0))
        coarse = mm(first_ref[...], jnp.concatenate(cols, 1))
        for which in range(2):
            real = coarse[:KP, which * FINE : (which + 1) * FINE]
            imag = coarse[KP:, which * FINE : (which + 1) * FINE]
            row = (2 * pair + which) * KP
            work_ref[row : row + KP, :FINE] = real * cos_tw + imag * sin_tw
            work_ref[row : row + KP, FINE:] = imag * cos_tw - real * sin_tw
    spec_ref[...] = mm_table(work_ref[...], forward_ref)


def inverse_signal(work_ref, inverse_ref, twiddle_ref, last_ref):
    work_ref[...] = mm_table(work_ref[...], inverse_ref)
    cos_tw, sin_tw = twiddle_ref[0], twiddle_ref[1]
    chans = []
    for pair in range(CH // 2):
        cols = []
        for chan in (2 * pair, 2 * pair + 1):
            real = work_ref[chan * KP : (chan + 1) * KP, :FINE]
            imag = work_ref[chan * KP : (chan + 1) * KP, FINE:]
            cols.append(
                jnp.concatenate(
                    [real * cos_tw - imag * sin_tw, imag * cos_tw + real * sin_tw], 0
                )
            )
        high, low = halves(jnp.concatenate(cols, 1))
        out = mm(last_ref[0], high) + mm(last_ref[0], low) + mm(last_ref[1], high)
        for which in range(2):
            mine = out[:, which * FINE : (which + 1) * FINE]
            chans.append(jnp.concatenate([mine[:32], mine[32:]], 1))
    return jnp.swapaxes(jnp.stack(chans, 0), 0, 1)


def times(left_ref, right_ref, sign_left, out_ref):
    lr, li = left_ref[:, :FINE], left_ref[:, FINE:]
    rr, ri = right_ref[:, :FINE], right_ref[:, FINE:]
    if sign_left > 0:
        out_ref[:, :FINE] = lr * rr - li * ri
        out_ref[:, FINE:] = lr * ri + li * rr
    else:
        out_ref[:, :FINE] = lr * rr + li * ri
        out_ref[:, FINE:] = lr * ri - li * rr


def prep_kernel(key_ref, value_ref, filter_ref, out_ref):
    kv = (key_ref[...].astype(F32) * value_ref[...].astype(F32)).astype(BF)
    out_ref[:, 0] = kv.reshape(CTX, CH, LOC)
    out_ref[:, 1] = filter_ref[...].astype(BF).reshape(CTX, CH, LOC)


def conv_kernel(
    in_ref, first, forward, inverse, twiddle, last, out_ref, kv_spec, fil_spec, work, early
):
    forward_spectrum(in_ref[:, 0], first, forward, twiddle, work, kv_spec)
    early[0]()
    forward_spectrum(in_ref[:, 1], first, forward, twiddle, work, fil_spec)
    early[1]()
    times(fil_spec, kv_spec, 1, work)
    out_ref[...] = inverse_signal(work, inverse, twiddle, last).astype(BF)


def grad_kernel(
    in_ref, kv_spec, fil_spec, first, forward, inverse, twiddle, last, out_ref, spec, work
):
    forward_spectrum(in_ref[...], first, forward, twiddle, work, spec)
    times(fil_spec, spec, -1, work)
    out_ref[:, 0] = inverse_signal(work, inverse, twiddle, last).astype(BF)
    times(kv_spec, spec, -1, work)
    out_ref[:, 1] = inverse_signal(work, inverse, twiddle, last).astype(BF)


def staged(kernel, scalars, ins, outs, flushed):
    def body(*refs):
        at = scalars + ins
        far_in, far_out = refs[scalars:at], refs[at : at + outs]
        at += outs
        near_in, near_out = refs[at : at + ins], refs[at + ins : at + ins + outs]
        sems = refs[at + ins + outs]
        loads = [
            pltpu.make_async_copy(far_in[i], near_in[i], sems.at[i]) for i in range(ins)
        ]
        for load in loads:
            load.start()
        for load in loads:
            load.wait()
        stores = [
            pltpu.make_async_copy(near_out[i], far_out[i], sems.at[ins + i]) for i in range(outs)
        ]
        early = [stores[i].start for i in range(outs - flushed, outs)]
        extra = (early,) if flushed else ()
        kernel(*refs[:scalars], *near_in, *near_out, *refs[at + ins + outs + 1 :], *extra)
        for store in stores[: outs - flushed]:
            store.start()
        for store in stores:
            store.wait()

    return body


def call(kernel, outs, *args, scalars=0, scratch=(), name=None, us=3, flushed=0):
    arrays = args[scalars:]
    hbm = pl.BlockSpec(memory_space=pltpu.HBM)
    specs = [pl.BlockSpec(memory_space=pltpu.SMEM)] * scalars + [hbm] * len(arrays)
    return pl.pallas_call(
        staged(kernel, scalars, len(arrays), len(outs), flushed),
        out_shape=[jax.ShapeDtypeStruct(shape, dtype) for shape, dtype in outs],
        in_specs=specs,
        out_specs=[hbm] * len(outs),
        scratch_shapes=[pltpu.VMEM(arg.shape, arg.dtype) for arg in arrays]
        + [pltpu.VMEM(shape, dtype) for shape, dtype in outs]
        + [pltpu.SemaphoreType.DMA((len(arrays) + len(outs),))]
        + list(scratch),
        compiler_params=pltpu.CompilerParams(vmem_limit_bytes=60 * MIB),
        cost_estimate=pl.CostEstimate(
            flops=us * 10**9, bytes_accessed=us * 3 * 10**6, transcendentals=0
        ),
        name=name,
    )(*args)


def inner_kernel(place_ref, weight_hbm, query_hbm, *refs):
    pieces_hbm, refs = refs[:TP], refs[TP:]
    inner_hbm, gated_hbm, keep_hbm, send_hbm = refs[:4]
    weight, pieces, query, inner_ref, gated_ref, load_sem, query_sem, store_sem = refs[4:]
    core = place_ref[TP]
    loads = []
    for idx in range(TP):
        begin = pl.multiple_of(place_ref[idx] * 512, 512)
        loads.append(
            [
                pltpu.make_async_copy(
                    weight_hbm.at[:, pl.ds(begin, 512)], weight.at[idx], load_sem.at[2 * idx]
                ),
                pltpu.make_async_copy(
                    pieces_hbm[idx], pieces.at[idx], load_sem.at[2 * idx + 1]
                ),
            ]
        )
        for load in loads[-1]:
            load.start()
    query_load = pltpu.make_async_copy(query_hbm, query, query_sem)
    query_load.start()
    total = jnp.zeros((ROWS, LOC), F32)
    stores = []
    for idx in range(TP):
        for load in loads[idx]:
            load.wait()
        total = total + mm(weight[idx], pieces[idx])
        for pair in range(2):
            slot = 2 * place_ref[idx] + pair
            mine = pl.multiple_of(pair * 256 + core * 128, 128)
            other = pl.multiple_of(pair * 256 + (1 - core) * 128, 128)
            for where, begin, kind in ((keep_hbm, mine, 0), (send_hbm, other, 1)):
                stores.append(
                    pltpu.make_async_copy(
                        pieces.at[idx, pl.ds(begin, 128)],
                        where.at[slot],
                        store_sem.at[4 * idx + 2 * pair + kind],
                    )
                )
                stores[-1].start()
    query_load.wait()
    inner = total.astype(BF)
    inner_ref[...] = inner
    gated_ref[...] = (inner.astype(F32) * query[...].astype(F32)).astype(BF)
    for near, far, sem in ((inner_ref, inner_hbm, 4 * TP), (gated_ref, gated_hbm, 4 * TP + 1)):
        stores.append(pltpu.make_async_copy(near, far, store_sem.at[sem]))
        stores[-1].start()
    for store in stores:
        store.wait()


def inner_call(place, weight_t, query, pieces):
    hbm = pl.BlockSpec(memory_space=pltpu.HBM)
    shapes = [(ROWS, LOC), (ROWS, LOC), (16, 128, LOC), (16, 128, LOC)]
    return pl.pallas_call(
        inner_kernel,
        out_shape=[jax.ShapeDtypeStruct(shape, BF) for shape in shapes],
        in_specs=[pl.BlockSpec(memory_space=pltpu.SMEM)] + [hbm] * (TP + 2),
        out_specs=[hbm] * 4,
        scratch_shapes=[
            pltpu.VMEM((TP, ROWS, 512), BF),
            pltpu.VMEM((TP, 512, LOC), BF),
            pltpu.VMEM((ROWS, LOC), BF),
            pltpu.VMEM((ROWS, LOC), BF),
            pltpu.VMEM((ROWS, LOC), BF),
            pltpu.SemaphoreType.DMA((2 * TP,)),
            pltpu.SemaphoreType.DMA,
            pltpu.SemaphoreType.DMA((4 * TP + 2,)),
        ],
        compiler_params=pltpu.CompilerParams(vmem_limit_bytes=60 * MIB),
        cost_estimate=pl.CostEstimate(
            flops=30 * 10**9, bytes_accessed=90 * 10**6, transcendentals=0
        ),
        name="inner",
    )(place, weight_t, query, *pieces)


def weight_kernel(place_ref, keep_ref, other_ref, mine_ref, sib_ref, own_ref, *outs):
    here = place_ref[0]
    for step in range(NX):
        want = lax.rem(here + step, NX)
        rows = jnp.concatenate(
            [
                jnp.concatenate([keep_ref[z * 4 + want], other_ref[z * 4 + want]], 1)
                for z in range(NZ)
            ],
            0,
        )
        cols = jnp.concatenate([mine_ref[...], sib_ref[...]], 1)
        part = lax.dot_general(
            rows, cols, (((1,), (1,)), ((), ())), preferred_element_type=F32
        ).reshape(NZ, 128, 512)
        if step == 0:
            own_ref[...] = part
        else:
            outs[step - 1][...] = part.astype(BF)


def fold_kernel(place_ref, own_ref, one_ref, two_ref, three_ref, mine_ref, *outs):
    here = place_ref[1]
    for step in range(NZ):
        want = lax.rem(here + step, NZ)
        total = (
            own_ref[want]
            + one_ref[want].astype(F32)
            + two_ref[want].astype(F32)
            + three_ref[want].astype(F32)
        )
        if step == 0:
            mine_ref[...] = total
        else:
            outs[step - 1][...] = total.astype(BF)


def post_kernel(back_ref, inner_ref, conv_ref, key_ref, value_ref, post_ref, halo_ref, corr_ref):
    kv_grad = back_ref[:, 0].reshape(ROWS, LOC).astype(F32)
    grads = (
        inner_ref[...].astype(F32) * conv_ref[...].astype(F32),
        kv_grad * value_ref[...].astype(F32),
        kv_grad * key_ref[...].astype(F32),
    )
    lane = lax.broadcasted_iota(jnp.int32, (ROWS, FINE), 1)
    halo = jnp.zeros((ROWS, FINE), F32)
    for which in range(3):
        rounded = grads[which].astype(BF)
        post_ref[which] = rounded
        head = rounded[:, :FINE].astype(F32)
        if which:
            head = pltpu.roll(head, 8 * which, 1)
        halo = jnp.where((lane >= 8 * which) & (lane < 8 * which + 8), head, halo)
    halo_ref[...] = halo.astype(BF)
    corr_ref[...] = back_ref[:, 1].reshape(ROWS, LOC).astype(F32)


def feature_kernel(post_ref, halo_ref, taps_ref, out_ref):
    halo = halo_ref[...].astype(F32)
    for which in range(3):
        tail = halo if which == 0 else pltpu.roll(halo, FINE - 8 * which, 1)
        wide = jnp.concatenate([post_ref[which].astype(F32), tail], 1)
        taps = jnp.concatenate([taps_ref[which], jnp.zeros((1, ROWS), F32)], 0).T
        total = taps[:, 0:1] * wide[:, :LOC]
        for offset in range(1, 7):
            moved = pltpu.roll(wide, LOC + FINE - offset, 1)
            total = total + taps[:, offset : offset + 1] * moved[:, :LOC]
        out_ref[which] = total.astype(BF)


def exchange(value):
    return lax.all_to_all(value, "ctx", split_axis=0, concat_axis=0, tiled=True)


def local(out_cotangent, query_rows, key_rows, value_rows, long_filter, short_filter, out_weight):
    ctx, tp = lax.axis_index("ctx"), lax.axis_index("tp")
    here_x, here_z, core = ctx // 2 % 4, ctx // 8, ctx % 2
    y, z_hi = tp // 2, tp % 2
    tables = [jnp.asarray(table) for table in make_tables()]

    far = lax.ppermute(out_cotangent, "tp", tp_shift(0, 1))
    near = [lax.ppermute(out_cotangent, "tp", tp_shift(step, 0)) for step in (1, 3, 2)]
    (sent,) = call(
        prep_kernel, [((CTX, 2, CH, LOC), BF)], key_rows, value_rows, long_filter, name="prep"
    )
    sent, far, *near = lax.optimization_barrier((sent, far, *near))
    pieces = [out_cotangent, far] + near
    pieces += [lax.ppermute(far, "tp", tp_shift(step, 0)) for step in (1, 3, 2)]
    sources = [tp, y * 2 + 1 - z_hi]
    for flip in (0, 1):
        for step in (1, 3, 2):
            sources.append((y + 4 - step) % 4 * 2 + (z_hi + flip) % 2)
    place = jnp.stack(sources + [core]).astype(jnp.int32)

    cols = exchange(sent)
    weight_t = out_weight.T
    spec_shape = ((CH * KP, 2 * FINE), F32)
    conv_cols, kv_spec, fil_spec = call(
        conv_kernel,
        [((CTX, CH, LOC), BF), spec_shape, spec_shape],
        cols,
        *tables,
        scratch=[pltpu.VMEM(*spec_shape)],
        name="conv",
        flushed=2,
        us=30,
    )
    conv_cols, place = lax.optimization_barrier((conv_cols, place))
    conv_out = exchange(conv_cols)
    inner, gated, keep, send = inner_call(place, weight_t, query_rows, pieces)
    conv_out, gated, send = lax.optimization_barrier((conv_out, gated, send))
    conv_out = conv_out.reshape(ROWS, LOC)
    gated_cols = exchange(gated.reshape(CTX, CH, LOC))
    other = lax.ppermute(send, "ctx", ctx_shift(0, 0, 1))
    mixed = (query_rows.astype(F32) * conv_out.astype(F32)).astype(BF)
    mixed_sib = lax.ppermute(mixed, "ctx", ctx_shift(0, 0, 1))
    spot = jnp.stack([here_x, here_z]).astype(jnp.int32)
    part = (NZ, 128, 512)
    own, *to_x = call(
        weight_kernel,
        [(part, F32)] + [(part, BF)] * 3,
        spot,
        keep,
        other,
        mixed,
        mixed_sib,
        scalars=1,
        name="weight",
    )
    from_x = [
        lax.ppermute(to_x[step - 1], "ctx", ctx_shift(0, step, 0)) for step in (1, 2, 3)
    ]

    gated_cols, own = lax.optimization_barrier((gated_cols, own))
    (back,) = call(
        grad_kernel,
        [((CTX, 2, CH, LOC), BF)],
        gated_cols,
        kv_spec,
        fil_spec,
        *tables,
        scratch=[pltpu.VMEM(*spec_shape), pltpu.VMEM(*spec_shape)],
        name="grad",
        us=5,
    )
    back = exchange(back)

    mine, *to_z = call(
        fold_kernel,
        [((128, 512), F32)] + [((128, 512), BF)] * 3,
        spot,
        own,
        *from_x,
        scalars=1,
        name="fold",
        us=30,
    )
    from_z = [
        lax.ppermute(to_z[step - 1], "ctx", ctx_shift(step, 0, 0)) for step in (1, 2, 3)
    ]
    back, mine = lax.optimization_barrier((back, mine))
    post, halo, filter_grad = call(
        post_kernel,
        [((3, ROWS, LOC), BF), ((ROWS, FINE), BF), ((ROWS, LOC), F32)],
        back,
        inner,
        conv_out,
        key_rows,
        value_rows,
        name="post",
    )
    halo = lax.ppermute(halo, "ctx", [(source, source - 1) for source in range(1, CTX)])
    (feature_grad,) = call(
        feature_kernel, [((3, ROWS, LOC), BF)], post, halo, short_filter.transpose(0, 2, 1), name="feature"
    )
    mine, feature_grad = lax.optimization_barrier((mine, feature_grad))
    out_weight_grad = mine + sum(value.astype(F32) for value in from_z)

    return (feature_grad, filter_grad, out_weight_grad)


def solution(mesh):
    return jax.shard_map(
        local,
        mesh=mesh,
        in_specs=(
            P("tp", "ctx"),
            P("tp", "ctx"),
            P("tp", "ctx"),
            P("tp", "ctx"),
            P("tp", "ctx"),
            P(None, "tp", None),
            P(None, "tp"),
        ),
        out_specs=(P(None, "tp", "ctx"), P("tp", "ctx"), P("ctx", "tp")),
        check_vma=False,
    )
```
